512 devices in a mesh: row: 16 (over x, z_lo), col: 32 (over z_hi, y, core).
Axes of the slice: x: 4, y: 4, z: 16 (z_hi: 4, z_lo: 4; z = z_hi * 4 + z_lo), core: 2. Of those that a mesh axis runs over, the one named last changes fastest.
Arguments:
- layer_input: bfloat16 [2048, 8192], P('row', 'col'), may hold values from -6 to 6
- rank_gate: bfloat16 [2048, 3072], P('col', 'row'), may hold values from -6 to 6
- rank_up: bfloat16 [2048, 3072], P('col', 'row'), may hold values from -6 to 6
- gate_pre: bfloat16 [2048, 29568], P('row', 'col'), may hold values from -12 to 12
- up_pre: bfloat16 [2048, 29568], P('row', 'col'), may hold values from -6 to 6
- hidden_grad: bfloat16 [2048, 29568], P('row', 'col'), may hold values from -0.59765625 to 0.59765625
- gate_inner: bfloat16 [8192, 3072], P('col', 'row'), may hold values from -0.0625 to 0.0625
- gate_outer: bfloat16 [3072, 29568], P('row', 'col'), may hold values from -0.109375 to 0.109375
- up_inner: bfloat16 [8192, 3072], P('col', 'row'), may hold values from -0.0625 to 0.0625
- up_outer: bfloat16 [3072, 29568], P('row', 'col'), may hold values from -0.109375 to 0.109375
Outputs:
- gate_inner_grad: float32 [8192, 3072], P('col', 'row')
- gate_outer_grad: float32 [3072, 29568], P('row', 'col')
- up_inner_grad: float32 [8192, 3072], P('col', 'row')
- up_outer_grad: float32 [3072, 29568], P('row', 'col')
- input_grad: bfloat16 [2048, 8192], P('row', 'col')
The draws below stay inside these ranges and needn't reach their ends.
All inputs are finite; a program needn't handle non-finite values.
Results may differ from the reference program's by a relative error of at most 0.03.
Values may be sent and summed in bfloat16 or wider, within the bound.
No kernel may reach another device: no remote copies, remote signals or barrier semaphores. Data moves between devices by JAX's collectives and lax.ppermute only.
A program may use at most 64 MiB of HBM per device.

```python
import jax
import jax.numpy as jnp
from jax import lax

D = 8192
FF = 29568
R = 3072
TOKENS = 2048
N_ROW = 16
N_COL = 32


def block_levels(own_key, dims, cuts, low, top_value):
    factor_of, own = 1.0, jax.random.fold_in(own_key, 6)
    for axis_at, shards_of in cuts:
        heights = jnp.exp(jax.random.uniform(jax.random.fold_in(own, axis_at), (shards_of,), jnp.float32, low / len(cuts), top_value / len(cuts)))
        factor_of = factor_of * jnp.repeat(heights, dims[axis_at] // shards_of).reshape([-1 if axis == axis_at else 1 for axis in range(len(dims))])
    return factor_of


def scatter_about(stream_key, extent, spread, limit, split=(), dtype=jnp.bfloat16):
    drawn = jax.random.normal(stream_key, extent, jnp.float32) * spread
    if len(split) > 0:
        drawn = block_levels(stream_key, extent, split, -0.22, 0.18) * drawn
    return jnp.clip(drawn, min=-limit, max=limit).astype(dtype)


def setup_inputs(seed: int = 0) -> dict:
    key_of = jax.random.split(jax.random.key(seed), 11)
    layer_input = scatter_about(key_of[0], (TOKENS, D), 1.0, 6.0, ((0, 16), (1, 32)))
    rank_gate = scatter_about(key_of[1], (TOKENS, R), 1.0, 6.0, ((0, 32), (1, 16)))
    rank_up = scatter_about(key_of[2], (TOKENS, R), 1.0, 6.0, ((0, 32), (1, 16)))
    gate_pre = scatter_about(key_of[3], (TOKENS, FF), 2.0, 12.0, ((0, 16), (1, 32)))
    up_pre = scatter_about(key_of[4], (TOKENS, FF), 1.0, 6.0, ((0, 16), (1, 32)))
    hidden_grad = scatter_about(key_of[5], (TOKENS, FF), 0.1, 0.59765625, ((0, 16), (1, 32)))
    gate_inner = scatter_about(key_of[6], (D, R), D ** -0.5, 0.0625, ((0, 32), (1, 16)))
    gate_outer = scatter_about(key_of[7], (R, FF), R ** -0.5, 0.109375, ((0, 16), (1, 32)))
    up_inner = scatter_about(key_of[8], (D, R), D ** -0.5, 0.0625, ((0, 32), (1, 16)))
    up_outer = scatter_about(key_of[9], (R, FF), R ** -0.5, 0.109375, ((0, 16), (1, 32)))
    return {"layer_input": layer_input, "rank_gate": rank_gate, "rank_up": rank_up, "gate_pre": gate_pre, "up_pre": up_pre, "hidden_grad": hidden_grad, "gate_inner": gate_inner, "gate_outer": gate_outer, "up_inner": up_inner, "up_outer": up_outer}


def swiglu_back(gate_pre, up_pre, hidden_grad):
    gate_val = gate_pre.astype(jnp.float32)
    up_val = up_pre.astype(jnp.float32)
    grad_val = hidden_grad.astype(jnp.float32)
    logistic = jax.nn.sigmoid(gate_val)
    gate_grad = (grad_val * up_val * logistic * (1.0 + gate_val * (1.0 - logistic))).astype(jnp.bfloat16)
    up_grad = (grad_val * gate_val * logistic).astype(jnp.bfloat16)
    return gate_grad, up_grad


def blocked_sum(lefts, rights, blocks):
    tokens = lefts[0].shape[0]
    outer = rights[0].shape[0]
    width = lefts[0].shape[1] // blocks

    def split_blocks(matrix):
        return matrix.reshape(matrix.shape[0], blocks, width).transpose(1, 0, 2)

    stacks = (tuple(split_blocks(m) for m in lefts), tuple(split_blocks(m) for m in rights))

    def advance(summed, pieces):
        left_blocks, right_blocks = pieces
        partial_value = jnp.zeros((tokens, outer), jnp.float32)
        for left_block, right_block in zip(left_blocks, right_blocks):
            partial_value = partial_value + jnp.dot(left_block, right_block.T, preferred_element_type=jnp.float32)
        rounded = lax.optimization_barrier(partial_value.astype(jnp.bfloat16))
        return summed + rounded.astype(jnp.float32), None

    summed, unused = lax.scan(advance, jnp.zeros((tokens, outer), jnp.float32), stacks)
    return summed


def reference(layer_input, rank_gate, rank_up, gate_pre, up_pre, hidden_grad, gate_inner, gate_outer, up_inner, up_outer):
    gate_grad, up_grad = swiglu_back(gate_pre, up_pre, hidden_grad)
    gate_outer_grad = jnp.dot(rank_gate.T, gate_grad, preferred_element_type=jnp.float32)
    up_outer_grad = jnp.dot(rank_up.T, up_grad, preferred_element_type=jnp.float32)
    rank_gate_grad = blocked_sum((gate_grad,), (gate_outer,), N_COL).astype(jnp.bfloat16)
    rank_up_grad = blocked_sum((up_grad,), (up_outer,), N_COL).astype(jnp.bfloat16)
    gate_inner_grad = jnp.dot(layer_input.T, rank_gate_grad, preferred_element_type=jnp.float32)
    up_inner_grad = jnp.dot(layer_input.T, rank_up_grad, preferred_element_type=jnp.float32)
    input_grad = blocked_sum((rank_gate_grad, rank_up_grad), (gate_inner, up_inner), N_ROW).astype(jnp.bfloat16)
    return gate_inner_grad, gate_outer_grad, up_inner_grad, up_outer_grad, input_grad
```

```python
import jax
import jax.numpy as jnp
from jax import lax
from jax.sharding import Mesh
from jax.sharding import PartitionSpec as P

F32 = jnp.float32
BF16 = jnp.bfloat16
RING = (0, 2, 3, 1)
SPOT = (0, 3, 1, 2)


def swiglu_back(gate_pre, up_pre, hidden_grad):
    gate_val = gate_pre.astype(F32)
    up_val = up_pre.astype(F32)
    grad_val = hidden_grad.astype(F32)
    logistic = jax.nn.sigmoid(gate_val)
    gate_grad = (grad_val * up_val * logistic * (1.0 + gate_val * (1.0 - logistic))).astype(BF16)
    up_grad = (grad_val * gate_val * logistic).astype(BF16)
    return (gate_grad, up_grad)


def turn(value, axis, step):
    return lax.ppermute(value, axis, [(i, (i + step) % 4) for i in range(4)])


def turn_z(value, step):
    return lax.ppermute(value, "zl", [(RING[i], RING[(i + step) % 4]) for i in range(4)])


def ring(value, move):
    blocks = [value]
    for _ in range(3):
        blocks.append(move(blocks[-1]))
    return blocks


def place_rank(rank, way):
    pairs = []
    for x in range(4):
        for zl in range(4):
            for zh in range(4):
                for y in range(4):
                    for c in range(2):
                        from_y = RING[(SPOT[zl] - y) % 4]
                        from_x = (x - way * zh) % 4
                        source = (((from_x * 4 + zl) * 4 + x) * 4 + from_y) * 2 + c
                        target = (((x * 4 + zl) * 4 + zh) * 4 + y) * 2 + c
                        pairs.append((source, target))
    return lax.ppermute(rank, ("x", "zl", "zh", "y", "c"), pairs)


def spread(value, axis):
    me = lax.axis_index(axis)
    stack = jnp.stack([value] + [turn(value, axis, k) for k in (1, 2, 3)])
    order = (me - jnp.arange(4)) % 4
    return stack[order]


def gather_rank(rank, way):
    piece = place_rank(rank, way)
    whole = lax.all_gather(piece, "zh")
    whole = lax.all_gather(whole, "y")
    whole = lax.all_gather(whole, "c")
    return whole.transpose(2, 1, 0, 3, 4).reshape(4, 512, 192)


def sum_over(value, axis):
    me = lax.axis_index(axis)
    total = lax.dynamic_index_in_dim(value, me, 0, keepdims=False)
    for k in (1, 2, 3):
        block = lax.dynamic_index_in_dim(value, (me + k) % 4, 0, keepdims=False)
        total = total + turn(block.astype(BF16), axis, k).astype(F32)
    return total


def reduce_col(part):
    me = lax.axis_index("c")
    halves = part.reshape(2, 256, 768)
    away = lax.dynamic_index_in_dim(halves, 1 - me, 0, keepdims=False).astype(BF16)
    mine = lax.dynamic_index_in_dim(halves, me, 0, keepdims=False)
    mine = mine + lax.ppermute(away, "c", [(0, 1), (1, 0)]).astype(F32)
    mine = sum_over(mine.reshape(4, 64, 768), "y")
    mine = sum_over(mine.reshape(4, 16, 768), "zh").astype(BF16)
    whole = lax.all_gather(mine, "zh", axis=0, tiled=True)
    whole = lax.all_gather(whole, "y", axis=0, tiled=True)
    return lax.all_gather(whole, "c", axis=0, tiled=True)


def on_device(
    layer_input,
    rank_gate,
    rank_up,
    gate_pre,
    up_pre,
    hidden_grad,
    gate_inner,
    gate_outer,
    up_inner,
    up_outer,
):
    gate_grad, up_grad = swiglu_back(gate_pre, up_pre, hidden_grad)
    ways = (1, -1)
    outers = [ring(w, lambda v, s=s: turn(v, "x", s)) for w, s in zip((gate_outer, up_outer), ways)]
    grads = [ring(g, lambda v: turn_z(v, 1)) for g in (gate_grad, up_grad)]
    ranks = [gather_rank(r, s) for r, s in zip((rank_gate, rank_up), ways)]
    inners = [ring(w, lambda v, s=s: turn(v, "x", s)) for w, s in zip((gate_inner, up_inner), ways)]
    inputs = jnp.concatenate(ring(layer_input, lambda v: turn_z(v, 1)), axis=0)

    outer_grads = []
    rank_grads = []
    for outer, grad, rank, way in zip(outers, grads, ranks, ways):
        grad = jnp.concatenate(grad, axis=0)
        outer = jnp.concatenate(outer, axis=0)
        part = jnp.einsum("tf,rf->tr", grad, outer, preferred_element_type=F32)
        rank_grads.append(reduce_col(part))
        total = jnp.einsum("tr,tf->rf", rank[0], grad, preferred_element_type=F32)
        for s in (1, 2, 3):
            other = jnp.einsum("tr,tf->rf", rank[s], grad, preferred_element_type=F32)
            total = total + turn(other.astype(BF16), "x", -s * way).astype(F32)
        outer_grads.append(total)

    inner_grads = []
    back = 0.0
    for inner, rank_grad, way in zip(inners, rank_grads, ways):
        inner = jnp.concatenate(inner, axis=1)
        back = back + jnp.einsum("tr,dr->td", rank_grad, inner, preferred_element_type=F32)
        part = jnp.einsum("td,tr->dr", inputs, rank_grad, preferred_element_type=F32)
        total = part[:, :192]
        for s in (1, 2, 3):
            other = part[:, 192 * s : 192 * (s + 1)].astype(BF16)
            total = total + turn(other, "x", -s * way).astype(F32)
        inner_grads.append(total)
    input_grad = back[:128]
    for s in (1, 2, 3):
        other = back[128 * s : 128 * (s + 1)].astype(BF16)
        input_grad = input_grad + turn_z(other, -s).astype(F32)
    return (
        inner_grads[0],
        outer_grads[0],
        inner_grads[1],
        outer_grads[1],
        input_grad.astype(BF16),
    )


def solution(mesh):
    grid = Mesh(mesh.devices.reshape(4, 4, 4, 4, 2), ("x", "zl", "zh", "y", "c"))
    row = ("x", "zl")
    col = ("zh", "y", "c")
    return jax.shard_map(
        on_device,
        mesh=grid,
        in_specs=(
            P(row, col),
            P(col, row),
            P(col, row),
            P(row, col),
            P(row, col),
            P(row, col),
            P(col, row),
            P(row, col),
            P(col, row),
            P(row, col),
        ),
        out_specs=(
            P(col, row),
            P(row, col),
            P(col, row),
            P(row, col),
            P(row, col),
        ),
        check_vma=False,
    )
```

```python
import jax
import jax.numpy as jnp
from jax import lax
from jax.experimental import pallas as pl
from jax.experimental.pallas import tpu as pltpu
from jax.sharding import Mesh
from jax.sharding import PartitionSpec as P

F32 = jnp.float32
BF16 = jnp.bfloat16
RING = (0, 2, 3, 1)
FF = 924
PAD = 928
WIDE = 1024


def swiglu_back(gate_pre, up_pre, hidden_grad):
    gate_val = gate_pre.astype(F32)
    up_val = up_pre.astype(F32)
    grad_val = hidden_grad.astype(F32)
    logistic = jax.nn.sigmoid(gate_val)
    gate_grad = (grad_val * up_val * logistic * (1.0 + gate_val * (1.0 - logistic))).astype(BF16)
    up_grad = (grad_val * gate_val * logistic).astype(BF16)
    return (gate_grad, up_grad)


def turn(value, axis, step):
    return lax.ppermute(value, axis, [(i, (i + step) % 4) for i in range(4)])


def turn_z(value, step):
    return lax.ppermute(value, "zl", [(RING[i], RING[(i + step) % 4]) for i in range(4)])


def exchange(value, axis):
    return lax.all_to_all(value, axis, 0, 0)


def kernel_call(body, out, vmem, rest=(), limit=48):
    def run(*refs):
        body(refs[: len(vmem)], refs[len(vmem) + len(rest) :])

    return pl.pallas_call(
        run,
        out_shape=[jax.ShapeDtypeStruct(shape, dtype) for shape, dtype in out],
        in_specs=[pl.BlockSpec(memory_space=pltpu.VMEM)] * len(vmem)
        + [pl.BlockSpec(memory_space=pl.ANY)] * len(rest),
        out_specs=[pl.BlockSpec(memory_space=pltpu.VMEM)] * len(out),
        compiler_params=pltpu.CompilerParams(vmem_limit_bytes=limit * 2**20),
        cost_estimate=pl.CostEstimate(flops=1000, bytes_accessed=1000, transcendentals=0),
    )(*vmem, *rest)


def dot(left, right, dims):
    return lax.dot_general(left, right, (dims, ((), ())), preferred_element_type=F32)


def z_owner(k):
    line = lax.axis_index("zl")
    spot = jnp.where(line == 0, 0, jnp.where(line == 1, 3, line - 1))
    place = (spot - k + 4) % 4
    return jnp.where(place == 0, 0, jnp.where(place == 3, 1, place + 1))


def factor_rows(refs, s, b, columns):
    if s == 2:
        return refs[2 + b][:, columns]
    return refs[{0: 0, 1: 1, 3: 4}[s]][192 * b : 192 * (b + 1), columns]


def join(met, rest):
    def body(ins, outs):
        for k in range(4):
            columns = slice(128 * k, 128 * (k + 1))
            outs[0][:, columns] = ins[k][: 2 * PAD, :]
            outs[1][:, columns] = ins[k][2 * PAD :, :]

    return kernel_call(body, [((2 * PAD, 512), BF16), ((256, 512), BF16)], met, rest)


def hidden_sums(grads, factors):
    def body(ins, outs):
        core = lax.axis_index("c")
        for b in range(2):
            grad = ins[0][0:WIDE, :] if b == 0 else ins[0][2 * PAD - WIDE :, :]
            for s in range(4):
                part = dot(factor_rows(ins[1:], s, b, slice(0, WIDE)), grad, ((1,), (0,))).astype(BF16)

                @pl.when(core == b)
                def _():
                    outs[1][192 * s : 192 * (s + 1), :] = part

                @pl.when(core != b)
                def _():
                    outs[0][192 * s : 192 * (s + 1), :] = part

                inner = factor_rows(ins[1:], s, b, slice(WIDE, WIDE + 256))
                outs[2][s, 192 * b : 192 * (b + 1), :] = inner

    out = [((768, 512), BF16)] * 2 + [((4, 384, 256), BF16)]
    return kernel_call(body, out, [grads, *factors])


def add(left, right, rest):
    def body(ins, outs):
        outs[0][...] = (ins[0][...].astype(F32) + ins[1][...].astype(F32)).astype(BF16)

    return kernel_call(body, [(left.shape, BF16)], [left, right], rest)[0]


def sum_blocks(value, copies, rest):
    shape = value.shape[1:]

    def body(ins, outs):
        total = (ins[0][0].astype(F32) + ins[0][1].astype(F32)) + (ins[0][2].astype(F32) + ins[0][3].astype(F32))
        if copies:
            for k in range(copies):
                outs[0][k] = total.astype(BF16)
        else:
            outs[0][...] = total.astype(BF16)

    return kernel_call(body, [((copies, *shape) if copies else shape, BF16)], [value], rest)[0]


def outer_sums(grads, rank, other):
    def body(ins, outs):
        first = lax.axis_index("c") == 0
        totals = [0.0, 0.0]
        for s in range(4):
            pieces = []
            for k in range(4):
                spot = (z_owner(k), s)
                mine, away = ins[1][spot], ins[2][spot]
                pieces.append(jnp.where(first, mine, away))
                pieces.append(jnp.where(first, away, mine))
            rank_rows = jnp.concatenate(pieces, axis=0)
            for b in range(2):
                left = rank_rows[:, 192 * b : 192 * (b + 1)]
                part = dot(left, ins[0][s, PAD * b : PAD * (b + 1), :], ((0,), (1,)))
                totals[b] = totals[b] + part
        for b in range(2):
            outs[b][...] = totals[b][:, :FF]

    return kernel_call(body, [((192, FF), F32)] * 2, [grads, rank, other])


def inner_sums(inputs, mine, away, rest):
    def body(ins, outs):
        core = lax.axis_index("c")
        me = lax.axis_index("x")
        for ref, branch in ((ins[1], core), (ins[2], 1 - core)):
            rows = pl.ds(pl.multiple_of(branch * 192, 16), 192)
            for s in range(4):
                part = dot(ref[192 * s : 192 * (s + 1), :], ins[0][...], ((1,), (1,)))
                outs[0][(me - s + 4) % 4, rows, :] = part.astype(BF16)

    return kernel_call(body, [((4, 384, 256), BF16)], [inputs, mine, away], rest)[0]


def input_sums(inner, mine, away, rest):
    def body(ins, outs):
        core = lax.axis_index("c")
        total = jnp.zeros((512, 256), F32)
        for ref, branch in ((ins[1], core), (ins[2], 1 - core)):
            rows = pl.ds(pl.multiple_of(branch * 192, 16), 192)
            for s in range(4):
                total = total + dot(ref[192 * s : 192 * (s + 1), :], ins[0][s, rows, :], ((0,), (0,)))
        for k in range(4):
            outs[0][z_owner(k)] = total[128 * k : 128 * (k + 1)].astype(BF16)

    return kernel_call(body, [((4, 128, 256), BF16)], [inner, mine, away], rest)[0]


def pack_factors(outers, inners):
    def body(ins, outs):
        for b in range(2):
            rows = slice(192 * b, 192 * (b + 1))
            ahead = b * (WIDE - PAD)
            parts = [ins[b][...], jnp.zeros((192, WIDE - FF - ahead), BF16)]
            if ahead:
                parts = [jnp.zeros((192, ahead), BF16), *parts]
            outs[0][rows, :WIDE] = jnp.concatenate(parts, axis=1)
            outs[0][rows, WIDE:] = ins[2 + b][...]

    return kernel_call(body, [((384, WIDE + 256), BF16)], [*outers, *inners])[0]


def gather_factors(value):
    back = turn(value, "x", 1)
    ahead = turn(value, "x", -1)
    return [value, back, turn(back[:192], "x", 1), turn(ahead[192:], "x", -1), ahead]


def after(value, rest):
    def body(ins, outs):
        outs[0][...] = ins[0][...]

    return kernel_call(body, [(value.shape, value.dtype)], [value], rest)[0]


def copies(value, rest):
    def body(ins, outs):
        for k in range(4):
            outs[0][k] = ins[0][...]

    return kernel_call(body, [((4, *value.shape), value.dtype)], [value], rest)[0]


def on_device(
    layer_input,
    rank_gate,
    rank_up,
    gate_pre,
    up_pre,
    hidden_grad,
    gate_inner,
    gate_outer,
    up_inner,
    up_outer,
):
    gate_grad, up_grad = swiglu_back(gate_pre.T, up_pre.T, hidden_grad.T)
    extra = ((0, PAD - FF), (0, 0))
    sent = jnp.concatenate((jnp.pad(gate_grad, extra), jnp.pad(up_grad, extra), layer_input.T), axis=0)
    back = turn_z(sent, 1)
    ahead = turn_z(sent, -1)
    met = [sent, back, turn_z(back, 1), ahead]
    factors = pack_factors((gate_outer, up_outer), (gate_inner.T, up_inner.T))
    factors = gather_factors(factors)
    rank = jnp.concatenate((rank_gate, rank_up), axis=1)

    grads, inputs = join(met, factors)
    away, mine, inner = hidden_sums(grads, factors)
    all_grads = lax.all_gather(grads, "x")
    mine = add(mine, lax.ppermute(away, "c", [(0, 1), (1, 0)]), [])
    rank = lax.all_gather(after(rank, [mine]), "zh")
    mine = exchange(mine.reshape(4, 192, 512), "y")
    mine = sum_blocks(mine, 0, [rank])
    rank = lax.all_gather(after(rank, [mine]), "y")
    mine = exchange(mine.reshape(4, 48, 512), "zh")
    mine = sum_blocks(mine, 4, [rank])
    mine = exchange(mine, "zh").reshape(192, 512)
    mine = exchange(copies(mine, []), "y").reshape(768, 512)
    away = lax.ppermute(mine, "c", [(0, 1), (1, 0)])

    inner_grads = jnp.sum(exchange(inner_sums(inputs, mine, away, []), "x").astype(F32), axis=0)
    input_grad = sum_blocks(exchange(input_sums(inner, mine, away, []), "zl"), 0, [])
    rank_other = lax.ppermute(rank, "c", [(0, 1), (1, 0)])
    outer_grads = outer_sums(all_grads, rank, rank_other)
    return (inner_grads[:192].T, outer_grads[0], inner_grads[192:].T, outer_grads[1], input_grad)


def solution(mesh):
    grid = Mesh(mesh.devices.reshape(4, 4, 4, 4, 2), ("x", "zl", "zh", "y", "c"))
    row = ("x", "zl")
    col = ("zh", "y", "c")
    return jax.shard_map(
        on_device,
        mesh=grid,
        in_specs=(
            P(row, col),
            P(col, row),
            P(col, row),
            P(row, col),
            P(row, col),
            P(row, col),
            P(col, row),
            P(row, col),
            P(col, row),
            P(row, col),
        ),
        out_specs=(
            P(col, row),
            P(row, col),
            P(col, row),
            P(row, col),
            P(row, col),
        ),
        check_vma=False,
    )
```

```python
import jax
import jax.numpy as jnp
from jax import lax
from jax.experimental import pallas as pl
from jax.experimental.pallas import tpu as pltpu
from jax.sharding import Mesh
from jax.sharding import PartitionSpec as P

F32 = jnp.float32
BF16 = jnp.bfloat16
RING = (0, 2, 3, 1)
FF = 924
PAD = 928
WIDE = 1024


def swiglu_back(gate_pre, up_pre, hidden_grad):
    gate_val = gate_pre.astype(F32)
    up_val = up_pre.astype(F32)
    grad_val = hidden_grad.astype(F32)
    logistic = jax.nn.sigmoid(gate_val)
    gate_grad = (grad_val * up_val * logistic * (1.0 + gate_val * (1.0 - logistic))).astype(BF16)
    up_grad = (grad_val * gate_val * logistic).astype(BF16)
    return (gate_grad, up_grad)


def turn(value, axis, step):
    return lax.ppermute(value, axis, [(i, (i + step) % 4) for i in range(4)])


def turn_z(value, step):
    return lax.ppermute(value, "zl", [(RING[i], RING[(i + step) % 4]) for i in range(4)])


def exchange(value, axis):
    return lax.all_to_all(value, axis, 0, 0)


def kernel_call(body, out, vmem, rest=(), near=(), limit=48):
    held = [*vmem, *near]

    def run(*refs):
        body(refs[: len(vmem)], refs[len(held) + len(rest) :])

    return pl.pallas_call(
        run,
        out_shape=[jax.ShapeDtypeStruct(shape, dtype) for shape, dtype in out],
        in_specs=[pl.BlockSpec(memory_space=pltpu.VMEM)] * len(held)
        + [pl.BlockSpec(memory_space=pl.ANY)] * len(rest),
        out_specs=[pl.BlockSpec(memory_space=pltpu.VMEM)] * len(out),
        compiler_params=pltpu.CompilerParams(vmem_limit_bytes=limit * 2**20),
        cost_estimate=pl.CostEstimate(flops=1000, bytes_accessed=1000, transcendentals=0),
    )(*held, *rest)


def dot(left, right, dims):
    return lax.dot_general(left, right, (dims, ((), ())), preferred_element_type=F32)


def z_owner(k):
    line = lax.axis_index("zl")
    spot = jnp.where(line == 0, 0, jnp.where(line == 1, 3, line - 1))
    place = (spot - k + 4) % 4
    return jnp.where(place == 0, 0, jnp.where(place == 3, 1, place + 1))


def copy_call(copies, out, scratch, arrays, rest, body=None, limit=48):
    n_in = len(arrays) + len(rest)

    def run(*refs):
        outs, held, sems = refs[n_in : n_in + len(out)], refs[n_in + len(out) : -1], refs[-1]
        pairs = copies(refs[: len(arrays)], outs, held)
        made = [pltpu.make_async_copy(source, target, sems.at[k]) for k, (source, target) in enumerate(pairs)]
        for copy in made:
            copy.start()
        if body is None:
            for copy in made:
                copy.wait()
        else:
            body(made, outs, *held)

    place = pl.ANY if body is None else pltpu.VMEM
    return pl.pallas_call(
        run,
        out_shape=[jax.ShapeDtypeStruct(shape, BF16) for shape in out],
        in_specs=[pl.BlockSpec(memory_space=pl.ANY)] * n_in,
        out_specs=[pl.BlockSpec(memory_space=place)] * len(out),
        scratch_shapes=[*scratch, pltpu.SemaphoreType.DMA((16,))],
        compiler_params=pltpu.CompilerParams(vmem_limit_bytes=limit * 2**20),
        cost_estimate=pl.CostEstimate(flops=1000, bytes_accessed=1000, transcendentals=0),
    )(*arrays, *rest)


def factor_rows(refs, s, rows, half, columns):
    if s == 2:
        return refs[2 + half].at[:, columns]
    return refs[{0: 0, 1: 1, 3: 4}[s]].at[rows, columns]


def hidden_sums(met, factors, branch, rest):
    def copies(ins, outs, held):
        grad_ref, outer_ref = held
        b = branch(lax.axis_index("c"))
        rows = pl.ds(pl.multiple_of(b * (2 * PAD - WIDE), 16), WIDE)
        pairs = [(ins[k].at[rows, :], grad_ref.at[:, 128 * k : 128 * (k + 1)]) for k in range(4)]
        rows = pl.ds(pl.multiple_of(b * 192, 16), 192)
        sources = [ins[4 + k].at[:, :WIDE] if k in (2, 3) else ins[4 + k].at[rows, :WIDE] for k in range(5)]
        return pairs + [(source, outer_ref.at[s]) for s, source in enumerate(sources)]

    def body(made, outs, grad_ref, outer_ref):
        for copy in made[:4]:
            copy.wait()
        for s, place in ((0, 0), (1, 1), (3, 4), (2, 2 + branch(lax.axis_index("c")))):
            for copy in {0: made[4:5], 1: made[5:6], 2: made[6:8], 3: made[8:9]}[s]:
                copy.wait()
            part = dot(outer_ref[place], grad_ref[...], ((1,), (0,)))
            outs[0][192 * s : 192 * (s + 1), :] = part.astype(BF16)

    scratch = [pltpu.VMEM((WIDE, 512), BF16), pltpu.VMEM((5, 192, WIDE), BF16)]
    return copy_call(copies, [(768, 512)], scratch, [*met, *factors], rest, body)[0]


def join(met, rest):
    def copies(ins, outs, held):
        return [(ins[k].at[: 2 * PAD, :], outs[0].at[:, 128 * k : 128 * (k + 1)]) for k in range(4)]

    return copy_call(copies, [(2 * PAD, 512)], [], met, rest)[0]


def join_inner(met, factors, rest):
    def copies(ins, outs, held):
        pairs = [(ins[k].at[2 * PAD :, :], outs[0].at[:, 128 * k : 128 * (k + 1)]) for k in range(4)]
        columns = slice(WIDE, WIDE + 256)
        for s in range(4):
            for b in range(2):
                rows = slice(192 * b, 192 * (b + 1))
                pairs.append((factor_rows(ins[4:], s, rows, b, columns), outs[1].at[s, rows, :]))
        return pairs

    return copy_call(copies, [(256, 512), (4, 384, 256)], [], [*met, *factors], rest)


def add(left, right, rest):
    def body(ins, outs):
        outs[0][...] = (ins[0][...].astype(F32) + ins[1][...].astype(F32)).astype(BF16)

    return kernel_call(body, [(left.shape, BF16)], [left, right], rest)[0]


def sum_blocks(value, copies, rest, near):
    shape = value.shape[1:]

    def body(ins, outs):
        total = (ins[0][0].astype(F32) + ins[0][1].astype(F32)) + (ins[0][2].astype(F32) + ins[0][3].astype(F32))
        for k in range(copies):
            outs[0][k] = total.astype(BF16)

    return kernel_call(body, [((copies, *shape), BF16)], [value], rest, near)[0]


def outer_sums(grads, rank, other, rest):
    def body(ins, outs):
        first = lax.axis_index("c") == 0
        totals = [0.0, 0.0]
        for x in range(4):
            pieces = []
            for k in range(4):
                spot = (z_owner(k), x)
                mine, away = ins[1][spot], ins[2][spot]
                pieces.append(jnp.where(first, mine, away))
                pieces.append(jnp.where(first, away, mine))
            rank_rows = jnp.concatenate(pieces, axis=0)
            for b in range(2):
                left = rank_rows[:, 192 * b : 192 * (b + 1)]
                part = dot(left, ins[0][x, PAD * b : PAD * (b + 1), :], ((0,), (1,)))
                totals[b] = totals[b] + part
        for b in range(2):
            outs[b][...] = totals[b][:, :FF]
        outs[2][...] = jnp.zeros((8, 128), F32)

    return kernel_call(body, [((192, FF), F32)] * 2 + [((8, 128), F32)], [grads, rank, other], rest)


def inner_total(value, rest):
    def body(ins, outs):
        for b in range(2):
            rows = slice(192 * b, 192 * (b + 1))
            low = ins[0][0, rows, :].astype(F32) + ins[0][1, rows, :].astype(F32)
            outs[b][...] = low + (ins[0][2, rows, :].astype(F32) + ins[0][3, rows, :].astype(F32))

    return kernel_call(body, [((192, 256), F32)] * 2, [value], rest)


def last_sums(inputs, inner, mine, away):
    def body(ins, outs):
        core = lax.axis_index("c")
        me = lax.axis_index("x")
        total = jnp.zeros((512, 256), F32)
        for ref, branch in ((ins[2], core), (ins[3], 1 - core)):
            rows = pl.ds(pl.multiple_of(branch * 192, 16), 192)
            for s in range(4):
                grad = ref[192 * s : 192 * (s + 1), :]
                outs[0][(me - s + 4) % 4, rows, :] = dot(grad, ins[0][...], ((1,), (1,))).astype(BF16)
                total = total + dot(grad, ins[1][s, rows, :], ((0,), (0,)))
        for k in range(4):
            outs[1 + k][...] = total[128 * k : 128 * (k + 1)].astype(outs[1 + k].dtype)

    out = [((4, 384, 256), BF16), ((128, 256), F32)] + [((128, 256), BF16)] * 3
    return kernel_call(body, out, [inputs, inner, mine, away])


def input_total(parts, rest):
    def body(ins, outs):
        total = ins[0][...] + ins[1][...].astype(F32)
        outs[0][...] = (total + (ins[2][...].astype(F32) + ins[3][...].astype(F32))).astype(BF16)

    return kernel_call(body, [((128, 256), BF16)], parts, rest)[0]


def pack_factors(outers, inners, rest):
    def body(ins, outs):
        for b in range(2):
            rows = slice(192 * b, 192 * (b + 1))
            ahead = b * (WIDE - PAD)
            parts = [ins[b][...], jnp.zeros((192, WIDE - FF - ahead), BF16)]
            if ahead:
                parts = [jnp.zeros((192, ahead), BF16), *parts]
            outs[0][rows, :WIDE] = jnp.concatenate(parts, axis=1)
            outs[0][rows, WIDE:] = ins[2 + b][...]

    return kernel_call(body, [((384, WIDE + 256), BF16)], [*outers, *inners], rest)[0]


def gather_factors(value):
    back = turn(value, "x", 1)
    ahead = turn(value, "x", -1)
    return [value, back, turn(back[:192], "x", 1), turn(ahead[192:], "x", -1), ahead]


def after(value, rest):
    def body(ins, outs):
        outs[0][...] = ins[0][...]

    return kernel_call(body, [(value.shape, value.dtype)], [value], rest)[0]


def on_device(
    layer_input,
    rank_gate,
    rank_up,
    gate_pre,
    up_pre,
    hidden_grad,
    gate_inner,
    gate_outer,
    up_inner,
    up_outer,
):
    gate_grad, up_grad = swiglu_back(gate_pre.T, up_pre.T, hidden_grad.T)
    extra = ((0, PAD - FF), (0, 0))
    sent = jnp.concatenate((jnp.pad(gate_grad, extra), jnp.pad(up_grad, extra), layer_input.T), axis=0)
    back = turn_z(sent, 1)
    ahead = turn_z(sent, -1)
    met = [sent, back, turn_z(back, 1), ahead]
    factors = pack_factors((gate_outer, up_outer), (gate_inner.T, up_inner.T), [sent])
    factors = gather_factors(factors)
    rank = jnp.concatenate((rank_gate, rank_up), axis=1)

    away = hidden_sums(met, factors, lambda core: 1 - core, [])
    grads = join(met, [away])
    all_grads = lax.all_gather(grads, "x")
    mine = hidden_sums(met, factors, lambda core: core, [grads])
    mine = add(mine, lax.ppermute(away, "c", [(0, 1), (1, 0)]), [])
    rank = lax.all_gather(after(rank, [mine]), "zh")
    mine = exchange(mine.reshape(4, 192, 512), "y")
    mine = sum_blocks(mine, 4, [], [rank])
    inputs, inner = join_inner(met, factors, [mine])
    rank = lax.all_gather(after(rank, [mine]), "y")
    rank_other = lax.ppermute(rank, "c", [(0, 1), (1, 0)])
    mine = exchange(mine, "zh")
    mine = sum_blocks(mine, 4, [], [rank_other, inputs])
    *outer_grads, token = outer_sums(all_grads, rank, rank_other, [mine])
    mine = after(exchange(mine, "y").reshape(768, 512), [token])
    away = lax.ppermute(mine, "c", [(0, 1), (1, 0)])

    inner_grads, *input_parts = last_sums(inputs, inner, mine, away)
    inner_grads = inner_total(exchange(inner_grads, "x"), [])
    input_grad = input_total([input_parts[0]] + [turn_z(input_parts[s], -s) for s in (1, 2, 3)], [])
    return (inner_grads[0].T, outer_grads[0], inner_grads[1].T, outer_grads[1], input_grad)


def solution(mesh):
    grid = Mesh(mesh.devices.reshape(4, 4, 4, 4, 2), ("x", "zl", "zh", "y", "c"))
    row = ("x", "zl")
    col = ("zh", "y", "c")
    return jax.shard_map(
        on_device,
        mesh=grid,
        in_specs=(
            P(row, col),
            P(col, row),
            P(col, row),
            P(row, col),
            P(row, col),
            P(row, col),
            P(col, row),
            P(row, col),
            P(col, row),
            P(row, col),
        ),
        out_specs=(
            P(col, row),
            P(row, col),
            P(col, row),
            P(row, col),
            P(row, col),
        ),
        check_vma=False,
    )
```

```python
import jax
import jax.numpy as jnp
from jax import lax
from jax.experimental import pallas as pl
from jax.experimental.pallas import tpu as pltpu
from jax.sharding import Mesh
from jax.sharding import PartitionSpec as P

F32 = jnp.float32
BF16 = jnp.bfloat16
RING = (0, 2, 3, 1)
FF = 924
PAD = 928
WIDE = 1024


def swiglu_back(gate_pre, up_pre, hidden_grad):
    gate_val = gate_pre.astype(F32)
    up_val = up_pre.astype(F32)
    grad_val = hidden_grad.astype(F32)
    logistic = jax.nn.sigmoid(gate_val)
    gate_grad = (grad_val * up_val * logistic * (1.0 + gate_val * (1.0 - logistic))).astype(BF16)
    up_grad = (grad_val * gate_val * logistic).astype(BF16)
    return (gate_grad, up_grad)


def turn(value, axis, step):
    return lax.ppermute(value, axis, [(i, (i + step) % 4) for i in range(4)])


def turn_z(value, step):
    return lax.ppermute(value, "zl", [(RING[i], RING[(i + step) % 4]) for i in range(4)])


def exchange(value, axis):
    return lax.all_to_all(value, axis, 0, 0)


def kernel_call(body, out, vmem, rest=(), near=(), limit=48):
    held = [*vmem, *near]

    def run(*refs):
        body(refs[: len(vmem)], refs[len(held) + len(rest) :])

    return pl.pallas_call(
        run,
        out_shape=[jax.ShapeDtypeStruct(shape, dtype) for shape, dtype in out],
        in_specs=[pl.BlockSpec(memory_space=pltpu.VMEM)] * len(held)
        + [pl.BlockSpec(memory_space=pl.ANY)] * len(rest),
        out_specs=[pl.BlockSpec(memory_space=pltpu.VMEM)] * len(out),
        compiler_params=pltpu.CompilerParams(vmem_limit_bytes=limit * 2**20),
        cost_estimate=pl.CostEstimate(flops=1000, bytes_accessed=1000, transcendentals=0),
    )(*held, *rest)


def dot(left, right, dims):
    return lax.dot_general(left, right, (dims, ((), ())), preferred_element_type=F32)


def z_owner(k):
    line = lax.axis_index("zl")
    spot = jnp.where(line == 0, 0, jnp.where(line == 1, 3, line - 1))
    place = (spot - k + 4) % 4
    return jnp.where(place == 0, 0, jnp.where(place == 3, 1, place + 1))


def copy_call(copies, out, scratch, arrays, rest, body=None, limit=48):
    n_in = len(arrays) + len(rest)

    def run(*refs):
        outs, held, sems = refs[n_in : n_in + len(out)], refs[n_in + len(out) : -1], refs[-1]
        pairs = copies(refs[: len(arrays)], outs, held)
        made = [pltpu.make_async_copy(source, target, sems.at[k]) for k, (source, target) in enumerate(pairs)]
        for copy in made:
            copy.start()
        if body is None:
            for copy in made:
                copy.wait()
        else:
            body(made, outs, *held)

    place = pl.ANY if body is None else pltpu.VMEM
    return pl.pallas_call(
        run,
        out_shape=[jax.ShapeDtypeStruct(shape, BF16) for shape in out],
        in_specs=[pl.BlockSpec(memory_space=pl.ANY)] * n_in,
        out_specs=[pl.BlockSpec(memory_space=place)] * len(out),
        scratch_shapes=[*scratch, pltpu.SemaphoreType.DMA((16,))],
        compiler_params=pltpu.CompilerParams(vmem_limit_bytes=limit * 2**20),
        cost_estimate=pl.CostEstimate(flops=1000, bytes_accessed=1000, transcendentals=0),
    )(*arrays, *rest)


def factor_rows(refs, s, rows, half, columns):
    if s == 2:
        return refs[2 + half].at[:, columns]
    return refs[{0: 0, 1: 1, 3: 4}[s]].at[rows, columns]


def hidden_sums(met, factors, branch, rest):
    def copies(ins, outs, held):
        grad_ref, outer_ref = held
        b = branch(lax.axis_index("c"))
        rows = pl.ds(pl.multiple_of(b * (2 * PAD - WIDE), 16), WIDE)
        pairs = [(ins[k].at[rows, :], grad_ref.at[:, 128 * k : 128 * (k + 1)]) for k in range(4)]
        rows = pl.ds(pl.multiple_of(b * 192, 16), 192)
        sources = [ins[4 + k].at[:, :WIDE] if k in (2, 3) else ins[4 + k].at[rows, :WIDE] for k in range(5)]
        return pairs + [(source, outer_ref.at[s]) for s, source in enumerate(sources)]

    def body(made, outs, grad_ref, outer_ref):
        for copy in made[:4]:
            copy.wait()
        for s, place in ((0, 0), (1, 1), (3, 4), (2, 2 + branch(lax.axis_index("c")))):
            for copy in {0: made[4:5], 1: made[5:6], 2: made[6:8], 3: made[8:9]}[s]:
                copy.wait()
            part = dot(outer_ref[place], grad_ref[...], ((1,), (0,)))
            outs[0][192 * s : 192 * (s + 1), :] = part.astype(BF16)

    scratch = [pltpu.VMEM((WIDE, 512), BF16), pltpu.VMEM((5, 192, WIDE), BF16)]
    return copy_call(copies, [(768, 512)], scratch, [*met, *factors], rest, body)[0]


def join(met, rest):
    def copies(ins, outs, held):
        return [(ins[k].at[: 2 * PAD, :], outs[0].at[:, 128 * k : 128 * (k + 1)]) for k in range(4)]

    return copy_call(copies, [(2 * PAD, 512)], [], met, rest)[0]


def join_inner(met, factors, rest):
    def copies(ins, outs, held):
        pairs = []
        for k in range(4):
            for half in range(2):
                start, place = 2 * PAD + 128 * half, slice(128 * half, 128 * (half + 1))
                pairs.append((ins[k].at[start : start + 128, :], outs[0].at[128 * k : 128 * (k + 1), place]))
        columns = slice(WIDE, WIDE + 256)
        for s in range(4):
            for b in range(2):
                rows = slice(192 * b, 192 * (b + 1))
                pairs.append((factor_rows(ins[4:], s, rows, b, columns), outs[1].at[s, rows, :]))
        return pairs

    return copy_call(copies, [(512, 256), (4, 384, 256)], [], [*met, *factors], rest)


def add(left, right, rest):
    def body(ins, outs):
        outs[0][...] = (ins[0][...].astype(F32) + ins[1][...].astype(F32)).astype(BF16)

    return kernel_call(body, [(left.shape, BF16)], [left, right], rest)[0]


def sum_blocks(value, copies, rest, near):
    shape = value.shape[1:]

    def body(ins, outs):
        total = (ins[0][0].astype(F32) + ins[0][1].astype(F32)) + (ins[0][2].astype(F32) + ins[0][3].astype(F32))
        for k in range(copies):
            outs[0][k] = total.astype(BF16)

    return kernel_call(body, [((copies, *shape), BF16)], [value], rest, near)[0]


def outer_sums(grads, rank, other, rest):
    def body(ins, outs):
        first = lax.axis_index("c") == 0
        totals = [0.0, 0.0]
        for x in range(4):
            pieces = []
            for k in range(4):
                spot = (z_owner(k), x)
                mine, away = ins[1][spot], ins[2][spot]
                pieces.append(jnp.where(first, mine, away))
                pieces.append(jnp.where(first, away, mine))
            rank_rows = jnp.concatenate(pieces, axis=0)
            for b in range(2):
                left = rank_rows[:, 192 * b : 192 * (b + 1)]
                part = dot(left, ins[0][x, PAD * b : PAD * (b + 1), :], ((0,), (1,)))
                totals[b] = totals[b] + part
        for b in range(2):
            outs[b][...] = totals[b][:, :FF]
        outs[2][...] = jnp.zeros((8, 128), F32)

    return kernel_call(body, [((192, FF), F32)] * 2 + [((8, 128), F32)], [grads, rank, other], rest)


def inner_total(value, rest):
    def body(ins, outs):
        for b in range(2):
            rows = slice(192 * b, 192 * (b + 1))
            low = ins[0][0, rows, :].astype(F32) + ins[0][1, rows, :].astype(F32)
            outs[b][...] = low + (ins[0][2, rows, :].astype(F32) + ins[0][3, rows, :].astype(F32))

    return kernel_call(body, [((192, 256), F32)] * 2, [value], rest)


def first_sums(inputs, inner, mine):
    def body(ins, outs):
        me = lax.axis_index("x")
        rows = pl.ds(pl.multiple_of(lax.axis_index("c") * 192, 16), 192)
        total = jnp.zeros((512, 256), F32)
        for s in range(4):
            grad = ins[2][192 * s : 192 * (s + 1), :]
            outs[0][(me - s + 4) % 4] = dot(grad, ins[0][...], ((1,), (0,))).astype(BF16)
            total = total + dot(grad, ins[1][s, rows, :], ((0,), (0,)))
        outs[1][...] = total

    return kernel_call(body, [((4, 192, 256), BF16), ((512, 256), F32)], [inputs, inner, mine])


def last_sums(inputs, inner, away, first, total):
    def body(ins, outs):
        core = lax.axis_index("c")
        me = lax.axis_index("x")
        here = pl.ds(pl.multiple_of(core * 192, 16), 192)
        rows = pl.ds(pl.multiple_of((1 - core) * 192, 16), 192)
        total = ins[4][...]
        for s in range(4):
            grad = ins[2][192 * s : 192 * (s + 1), :]
            outs[0][(me - s + 4) % 4, rows, :] = dot(grad, ins[0][...], ((1,), (0,))).astype(BF16)
            outs[0][s, here, :] = ins[3][s]
            total = total + dot(grad, ins[1][s, rows, :], ((0,), (0,)))
        for k in range(4):
            outs[1 + k][...] = total[128 * k : 128 * (k + 1)].astype(outs[1 + k].dtype)

    out = [((4, 384, 256), BF16), ((128, 256), F32)] + [((128, 256), BF16)] * 3
    return kernel_call(body, out, [inputs, inner, away, first, total])


def input_total(parts, rest):
    def body(ins, outs):
        total = ins[0][...] + ins[1][...].astype(F32)
        outs[0][...] = (total + (ins[2][...].astype(F32) + ins[3][...].astype(F32))).astype(BF16)

    return kernel_call(body, [((128, 256), BF16)], parts, rest)[0]


def pack_factors(outers, inners, rest):
    def body(ins, outs):
        for b in range(2):
            rows = slice(192 * b, 192 * (b + 1))
            ahead = b * (WIDE - PAD)
            parts = [ins[b][...], jnp.zeros((192, WIDE - FF - ahead), BF16)]
            if ahead:
                parts = [jnp.zeros((192, ahead), BF16), *parts]
            outs[0][rows, :WIDE] = jnp.concatenate(parts, axis=1)
            outs[0][rows, WIDE:] = ins[2 + b][...]

    return kernel_call(body, [((384, WIDE + 256), BF16)], [*outers, *inners], rest)[0]


def gather_factors(value):
    back = turn(value, "x", 1)
    ahead = turn(value, "x", -1)
    return [value, back, turn(back[:192], "x", 1), turn(ahead[192:], "x", -1), ahead]


def after(value, rest):
    def body(ins, outs):
        outs[0][...] = ins[0][...]

    return kernel_call(body, [(value.shape, value.dtype)], [value], rest)[0]


def on_device(
    layer_input,
    rank_gate,
    rank_up,
    gate_pre,
    up_pre,
    hidden_grad,
    gate_inner,
    gate_outer,
    up_inner,
    up_outer,
):
    gate_grad, up_grad = swiglu_back(gate_pre.T, up_pre.T, hidden_grad.T)
    extra = ((0, PAD - FF), (0, 0))
    sent = jnp.concatenate((jnp.pad(gate_grad, extra), jnp.pad(up_grad, extra), *jnp.split(layer_input, 2, axis=1)), axis=0)
    back = turn_z(sent, 1)
    ahead = turn_z(sent, -1)
    met = [sent, back, turn_z(back, 1), ahead]
    factors = pack_factors((gate_outer, up_outer), (gate_inner.T, up_inner.T), [sent])
    factors = gather_factors(factors)
    rank = jnp.concatenate((rank_gate, rank_up), axis=1)

    away = hidden_sums(met, factors, lambda core: 1 - core, [])
    grads = join(met, [away])
    all_grads = lax.all_gather(grads, "x")
    mine = hidden_sums(met, factors, lambda core: core, [grads])
    mine = add(mine, lax.ppermute(away, "c", [(0, 1), (1, 0)]), [])
    rank = lax.all_gather(after(rank, [mine]), "zh")
    mine = exchange(mine.reshape(4, 192, 512), "y")
    mine = sum_blocks(mine, 4, [], [rank])
    inputs, inner = join_inner(met, factors, [mine])
    rank = lax.all_gather(after(rank, [mine]), "y")
    rank_other = lax.ppermute(rank, "c", [(0, 1), (1, 0)])
    mine = exchange(mine, "zh")
    mine = sum_blocks(mine, 4, [rank_other], [inputs])
    *outer_grads, token = outer_sums(all_grads, rank, rank_other, [mine])
    mine = after(exchange(mine, "y").reshape(768, 512), [token])
    away = lax.ppermute(mine, "c", [(0, 1), (1, 0)])

    first, total = first_sums(inputs, inner, mine)
    inner_grads, *input_parts = last_sums(inputs, inner, away, first, total)
    inner_grads = inner_total(exchange(inner_grads, "x"), [])
    input_grad = input_total([input_parts[0]] + [turn_z(input_parts[s], -s) for s in (1, 2, 3)], [])
    return (inner_grads[0].T, outer_grads[0], inner_grads[1].T, outer_grads[1], input_grad)


def solution(mesh):
    grid = Mesh(mesh.devices.reshape(4, 4, 4, 4, 2), ("x", "zl", "zh", "y", "c"))
    row = ("x", "zl")
    col = ("zh", "y", "c")
    return jax.shard_map(
        on_device,
        mesh=grid,
        in_specs=(
            P(row, col),
            P(col, row),
            P(col, row),
            P(row, col),
            P(row, col),
            P(row, col),
            P(col, row),
            P(row, col),
            P(col, row),
            P(row, col),
        ),
        out_specs=(
            P(col, row),
            P(row, col),
            P(col, row),
            P(row, col),
            P(row, col),
        ),
        check_vma=False,
    )
```

```python
import jax
import jax.numpy as jnp
from jax import lax
from jax.experimental import pallas as pl
from jax.experimental.pallas import tpu as pltpu
from jax.sharding import Mesh
from jax.sharding import PartitionSpec as P

F32 = jnp.float32
BF16 = jnp.bfloat16
RING = (0, 2, 3, 1)
FF = 924
PAD = 928
WIDE = 1024


def swiglu_back(gate_pre, up_pre, hidden_grad):
    gate_val = gate_pre.astype(F32)
    up_val = up_pre.astype(F32)
    grad_val = hidden_grad.astype(F32)
    logistic = jax.nn.sigmoid(gate_val)
    gate_grad = (grad_val * up_val * logistic * (1.0 + gate_val * (1.0 - logistic))).astype(BF16)
    up_grad = (grad_val * gate_val * logistic).astype(BF16)
    return (gate_grad, up_grad)


def turn(value, axis, step):
    return lax.ppermute(value, axis, [(i, (i + step) % 4) for i in range(4)])


def turn_z(value, step):
    return lax.ppermute(value, "zl", [(RING[i], RING[(i + step) % 4]) for i in range(4)])


def exchange(value, axis):
    return lax.all_to_all(value, axis, 0, 0)


def kernel_call(body, out, vmem, rest=(), near=(), limit=48):
    held = [*vmem, *near]

    def run(*refs):
        body(refs[: len(vmem)], refs[len(held) + len(rest) :])

    return pl.pallas_call(
        run,
        out_shape=[jax.ShapeDtypeStruct(shape, dtype) for shape, dtype in out],
        in_specs=[pl.BlockSpec(memory_space=pltpu.VMEM)] * len(held)
        + [pl.BlockSpec(memory_space=pl.ANY)] * len(rest),
        out_specs=[pl.BlockSpec(memory_space=pltpu.VMEM)] * len(out),
        compiler_params=pltpu.CompilerParams(vmem_limit_bytes=limit * 2**20),
        cost_estimate=pl.CostEstimate(flops=1000, bytes_accessed=1000, transcendentals=0),
    )(*held, *rest)


def dot(left, right, dims):
    return lax.dot_general(left, right, (dims, ((), ())), preferred_element_type=F32)


def z_owner(k):
    line = lax.axis_index("zl")
    spot = jnp.where(line == 0, 0, jnp.where(line == 1, 3, line - 1))
    place = (spot - k + 4) % 4
    return jnp.where(place == 0, 0, jnp.where(place == 3, 1, place + 1))


def copy_call(copies, out, scratch, arrays, rest, body=None, limit=48):
    n_in = len(arrays) + len(rest)

    def run(*refs):
        outs, held, sems = refs[n_in : n_in + len(out)], refs[n_in + len(out) : -1], refs[-1]
        pairs = copies(refs[: len(arrays)], outs, held)
        made = [pltpu.make_async_copy(source, target, sems.at[k]) for k, (source, target) in enumerate(pairs)]
        for copy in made:
            copy.start()
        if body is None:
            for copy in made:
                copy.wait()
        else:
            body(made, outs, *held)

    place = pl.ANY if body is None else pltpu.VMEM
    return pl.pallas_call(
        run,
        out_shape=[jax.ShapeDtypeStruct(shape, BF16) for shape in out],
        in_specs=[pl.BlockSpec(memory_space=pl.ANY)] * n_in,
        out_specs=[pl.BlockSpec(memory_space=place)] * len(out),
        scratch_shapes=[*scratch, pltpu.SemaphoreType.DMA((16,))],
        compiler_params=pltpu.CompilerParams(vmem_limit_bytes=limit * 2**20),
        cost_estimate=pl.CostEstimate(flops=1000, bytes_accessed=1000, transcendentals=0),
    )(*arrays, *rest)


def factor_rows(refs, s, rows, half, columns):
    if s == 2:
        return refs[2 + half].at[:, columns]
    return refs[{0: 0, 1: 1, 3: 4}[s]].at[rows, columns]


def hidden_sums(met, factors, branch, rest):
    def copies(ins, outs, held):
        grad_ref, outer_ref = held
        b = branch(lax.axis_index("c"))
        rows = pl.ds(pl.multiple_of(b * (2 * PAD - WIDE), 16), WIDE)
        pairs = [(ins[k].at[rows, :], grad_ref.at[:, 128 * k : 128 * (k + 1)]) for k in range(4)]
        rows = pl.ds(pl.multiple_of(b * 192, 16), 192)
        sources = [ins[4 + k].at[:, :WIDE] if k in (2, 3) else ins[4 + k].at[rows, :WIDE] for k in range(5)]
        return pairs + [(source, outer_ref.at[s]) for s, source in enumerate(sources)]

    def body(made, outs, grad_ref, outer_ref):
        for copy in made[:4]:
            copy.wait()
        for s, place in ((0, 0), (1, 1), (3, 4), (2, 2 + branch(lax.axis_index("c")))):
            for copy in {0: made[4:5], 1: made[5:6], 2: made[6:8], 3: made[8:9]}[s]:
                copy.wait()
            part = dot(outer_ref[place], grad_ref[...], ((1,), (0,)))
            outs[0][192 * s : 192 * (s + 1), :] = part.astype(BF16)

    scratch = [pltpu.VMEM((WIDE, 512), BF16), pltpu.VMEM((5, 192, WIDE), BF16)]
    return copy_call(copies, [(768, 512)], scratch, [*met, *factors], rest, body)[0]


def join(met, rest):
    def copies(ins, outs, held):
        return [(ins[k].at[: 2 * PAD, :], outs[0].at[:, 128 * k : 128 * (k + 1)]) for k in range(4)]

    return copy_call(copies, [(2 * PAD, 512)], [], met, rest)[0]


def join_inner(met, factors, rest):
    def copies(ins, outs, held):
        pairs = []
        for k in range(4):
            for half in range(2):
                start, place = 2 * PAD + 128 * half, slice(128 * half, 128 * (half + 1))
                pairs.append((ins[k].at[start : start + 128, :], outs[0].at[128 * k : 128 * (k + 1), place]))
        columns = slice(WIDE, WIDE + 256)
        for s in range(4):
            for b in range(2):
                rows = slice(192 * b, 192 * (b + 1))
                pairs.append((factor_rows(ins[4:], s, rows, b, columns), outs[1].at[s, rows, :]))
        return pairs

    return copy_call(copies, [(512, 256), (4, 384, 256)], [], [*met, *factors], rest)


def add(left, right, rest):
    def body(ins, outs):
        outs[0][...] = (ins[0][...].astype(F32) + ins[1][...].astype(F32)).astype(BF16)

    return kernel_call(body, [(left.shape, BF16)], [left, right], rest)[0]


def sum_blocks(value, copies, rest, near):
    shape = value.shape[1:]

    def body(ins, outs):
        total = (ins[0][0].astype(F32) + ins[0][1].astype(F32)) + (ins[0][2].astype(F32) + ins[0][3].astype(F32))
        for k in range(copies):
            outs[0][k] = total.astype(BF16)

    return kernel_call(body, [((copies, *shape), BF16)], [value], rest, near)[0]


def outer_sums(grads, rank, other, rest):
    def body(ins, outs):
        first = lax.axis_index("c") == 0
        totals = [0.0, 0.0]
        for x in range(4):
            pieces = []
            for k in range(4):
                spot = (z_owner(k), x)
                mine, away = ins[1][spot], ins[2][spot]
                pieces.append(jnp.where(first, mine, away))
                pieces.append(jnp.where(first, away, mine))
            rank_rows = jnp.concatenate(pieces, axis=0)
            for b in range(2):
                left = rank_rows[:, 192 * b : 192 * (b + 1)]
                part = dot(left, ins[0][x, PAD * b : PAD * (b + 1), :], ((0,), (1,)))
                totals[b] = totals[b] + part
        for b in range(2):
            outs[b][...] = totals[b][:, :FF]
        outs[2][...] = jnp.zeros((8, 128), F32)

    return kernel_call(body, [((192, FF), F32)] * 2 + [((8, 128), F32)], [grads, rank, other], rest)


def inner_total(value, rest):
    def body(ins, outs):
        for b in range(2):
            rows = slice(192 * b, 192 * (b + 1))
            low = ins[0][0, rows, :].astype(F32) + ins[0][1, rows, :].astype(F32)
            outs[b][...] = low + (ins[0][2, rows, :].astype(F32) + ins[0][3, rows, :].astype(F32))

    return kernel_call(body, [((192, 256), F32)] * 2, [value], rest)


def first_sums(inputs, inner, mine):
    def body(ins, outs):
        me = lax.axis_index("x")
        rows = pl.ds(pl.multiple_of(lax.axis_index("c") * 192, 16), 192)
        total = jnp.zeros((512, 256), F32)
        for s in range(4):
            grad = ins[2][192 * s : 192 * (s + 1), :]
            outs[0][(me - s + 4) % 4] = dot(grad, ins[0][...], ((1,), (0,))).astype(BF16)
            total = total + dot(grad, ins[1][s, rows, :], ((0,), (0,)))
        outs[1][...] = total

    return kernel_call(body, [((4, 192, 256), BF16), ((512, 256), F32)], [inputs, inner, mine])


def last_sums(inputs, inner, away, first, total):
    def body(ins, outs):
        core = lax.axis_index("c")
        me = lax.axis_index("x")
        here = pl.ds(pl.multiple_of(core * 192, 16), 192)
        rows = pl.ds(pl.multiple_of((1 - core) * 192, 16), 192)
        total = ins[4][...]
        for s in range(4):
            grad = ins[2][192 * s : 192 * (s + 1), :]
            outs[0][(me - s + 4) % 4, rows, :] = dot(grad, ins[0][...], ((1,), (0,))).astype(BF16)
            outs[0][s, here, :] = ins[3][s]
            total = total + dot(grad, ins[1][s, rows, :], ((0,), (0,)))
        for k in range(4):
            outs[1 + k][...] = total[128 * k : 128 * (k + 1)].astype(outs[1 + k].dtype)

    out = [((4, 384, 256), BF16), ((128, 256), F32)] + [((128, 256), BF16)] * 3
    return kernel_call(body, out, [inputs, inner, away, first, total])


def input_total(parts, rest):
    def body(ins, outs):
        total = ins[0][...] + ins[1][...].astype(F32)
        outs[0][...] = (total + (ins[2][...].astype(F32) + ins[3][...].astype(F32))).astype(BF16)

    return kernel_call(body, [((128, 256), BF16)], parts, rest)[0]


def pack_factors(outers, inners, rest):
    def body(ins, outs):
        for b in range(2):
            rows = slice(192 * b, 192 * (b + 1))
            ahead = b * (WIDE - PAD)
            parts = [ins[b][...], jnp.zeros((192, WIDE - FF - ahead), BF16)]
            if ahead:
                parts = [jnp.zeros((192, ahead), BF16), *parts]
            outs[0][rows, :WIDE] = jnp.concatenate(parts, axis=1)
            outs[0][rows, WIDE:] = ins[2 + b][...]

    return kernel_call(body, [((384, WIDE + 256), BF16)], [*outers, *inners], rest)[0]


def gather_factors(value):
    back = turn(value, "x", 1)
    ahead = turn(value, "x", -1)
    return [value, back, turn(back[:192], "x", 1), turn(ahead[192:], "x", -1), ahead]


def after(value, rest):
    def body(ins, outs):
        outs[0][...] = ins[0][...]

    return kernel_call(body, [(value.shape, value.dtype)], [value], rest)[0]


def on_device(
    layer_input,
    rank_gate,
    rank_up,
    gate_pre,
    up_pre,
    hidden_grad,
    gate_inner,
    gate_outer,
    up_inner,
    up_outer,
):
    gate_grad, up_grad = swiglu_back(gate_pre.T, up_pre.T, hidden_grad.T)
    extra = ((0, PAD - FF), (0, 0))
    sent = jnp.concatenate((jnp.pad(gate_grad, extra), jnp.pad(up_grad, extra), *jnp.split(layer_input, 2, axis=1)), axis=0)
    back = turn_z(sent, 1)
    ahead = turn_z(sent, -1)
    met = [sent, back, turn_z(back, 1), ahead]
    factors = pack_factors((gate_outer, up_outer), (gate_inner.T, up_inner.T), [sent])
    factors = gather_factors(factors)
    rank = jnp.concatenate((rank_gate, rank_up), axis=1)

    away = hidden_sums(met, factors, lambda core: 1 - core, [])
    grads = join(met, [away])
    all_grads = lax.all_gather(grads, "x")
    mine = hidden_sums(met, factors, lambda core: core, [grads])
    mine = add(mine, lax.ppermute(away, "c", [(0, 1), (1, 0)]), [])
    rank = lax.all_gather(after(rank, [mine]), "zh")
    mine = exchange(mine.reshape(4, 192, 512), "y")
    mine = sum_blocks(mine, 4, [], [rank])
    inputs, inner = join_inner(met, factors, [mine])
    rank = lax.all_gather(after(rank, [mine]), "y")
    rank_other = lax.ppermute(rank, "c", [(0, 1), (1, 0)])
    mine = exchange(mine, "zh")
    mine = sum_blocks(mine, 4, [], [inputs])
    *outer_grads, token = outer_sums(all_grads, rank, rank_other, [mine])
    mine = after(exchange(mine, "y").reshape(768, 512), [token])
    away = lax.ppermute(mine, "c", [(0, 1), (1, 0)])

    first, total = first_sums(inputs, inner, mine)
    inner_grads, *input_parts = last_sums(inputs, inner, away, first, total)
    inner_grads = inner_total(exchange(inner_grads, "x"), [])
    input_grad = input_total([input_parts[0]] + [turn_z(input_parts[s], -s) for s in (1, 2, 3)], [])
    return (inner_grads[0].T, outer_grads[0], inner_grads[1].T, outer_grads[1], input_grad)


def solution(mesh):
    grid = Mesh(mesh.devices.reshape(4, 4, 4, 4, 2), ("x", "zl", "zh", "y", "c"))
    row = ("x", "zl")
    col = ("zh", "y", "c")
    return jax.shard_map(
        on_device,
        mesh=grid,
        in_specs=(
            P(row, col),
            P(col, row),
            P(col, row),
            P(row, col),
            P(row, col),
            P(row, col),
            P(col, row),
            P(row, col),
            P(col, row),
            P(row, col),
        ),
        out_specs=(
            P(col, row),
            P(row, col),
            P(col, row),
            P(row, col),
            P(row, col),
        ),
        check_vma=False,
    )
```
